32 devices in a mesh: person: 4 (over z), var: 8 (over y, x, core).
Axes of the slice: x: 2, y: 2, z: 4, core: 2. Of those that a mesh axis runs over, the one named last changes fastest.
Arguments:
- linear_pred: float32 [64, 12288], P('var', 'person'), may hold values from -3 to 3
- event_flag: int32 [12288], P('person'), may hold values 0 or 1
- fold_id: int32 [12288], P('person'), may hold values from 0 to 7
- tie_group: int32 [12288], P('person'), may hold values from 0 to 12287, as said below
- time_order: int32 [12288], P('person'), may hold values from 0 to 12287, as said below
- genotypes: int32 [2048, 16384], P('person', 'var'), may hold values from 0 to 728, as said below
- variant_scale: float32 [16384], P('var'), may hold values from 1 to 4
- penalty: float32 [64], P('person'), may hold values from 0.3 to 3
- strong_set: int32 [64, 16384], P('person', 'var'), may hold values 0 or 1
Outputs:
- gradient: float32 [64, 16384], P('person', 'var')
- violation: float32 [64, 16384], P('person', 'var')
The draws below stay inside these ranges and needn't reach their ends.
Inputs may be any that keep to these rules, and one draw needn't show every extreme that they name: `time_order`: A permutation. Each aligned block of 3072 consecutive event-time ranks holds exactly 768 persons of each aligned block of 3072 file positions. `tie_group`: never falls along event-time rank; each group is consecutive ranks inside one aligned block of 3072 ranks, holds at most 4 persons, and some group of every block holds exactly 4. `genotypes`: word r of a variant holds the allele counts (0, 1 or 2) of file persons 6 r to 6 r + 5 as base-3 digits, person 6 r + s with weight 3 ** s.
All inputs are finite; a program needn't handle non-finite values. No bound on the sum of `event_flag` or of `strong_set` on one device may be relied on, other than what follows from the above.
Results may differ from the reference program's by a relative error of at most 0.0036.
The reference program's roundings to bfloat16 on the way (of `resid`, `in_file` and `dosage`) count: a program that leaves them out, or rounds other values in their place, can miss the bound.
Values may be sent and summed in bfloat16 or wider, within the bound.
A program may use at most 64 MiB of HBM per device.

```python
import math
import jax
import jax.numpy as jnp
from jax import lax

K = 64
FOLDS = 8
TIE_MAX = 4
P_DEV = 3072
PERSONS = 12288
VARIANTS = 16384
WORDS = 2048
N_PERSON = 4


def draw_time_order(key, part):
    key = jax.random.fold_in(key, 11)
    first_key, second_key = jax.random.split(key)
    share = P_DEV // N_PERSON
    within = jax.vmap(lambda one: jax.random.permutation(one, P_DEV))(jax.random.split(first_key, N_PERSON))
    grouped = within.reshape(N_PERSON, N_PERSON, share) + (jnp.arange(N_PERSON, dtype=jnp.int32) * P_DEV)[:, None, None]
    per_time = grouped.transpose(1, 0, 2).reshape(N_PERSON, P_DEV)
    mixed = jax.vmap(lambda one, row: jax.random.permutation(one, row))(jax.random.split(second_key, N_PERSON), per_time)
    return mixed.reshape(-1).astype(jnp.int32)


def draw_tie_group(key, part):
    key = jax.random.fold_in(key, 12)
    lengths = jax.random.randint(key, (N_PERSON, P_DEV), 1, TIE_MAX + 1)
    lengths = lengths.at[:, 0].set(TIE_MAX)
    starts = jnp.cumsum(lengths, axis=1) - lengths
    places = jnp.arange(P_DEV, dtype=jnp.int32)
    local = jax.vmap(lambda row: jnp.searchsorted(row, places, side='right'))(starts) - 1
    offsets = (jnp.arange(N_PERSON, dtype=jnp.int32) * P_DEV)[:, None]
    return (local.astype(jnp.int32) + offsets).reshape(-1).astype(jnp.int32)


def draw_genotypes(key, part):
    key = jax.random.fold_in(key, 13)
    rate_key, count_key = jax.random.split(key)
    rate = jax.random.randint(rate_key, (1, VARIANTS), 20, 500)
    packed = jnp.zeros((WORDS, VARIANTS), jnp.int32)
    for member in range(6):
        uniform_pair = jax.random.randint(jax.random.fold_in(count_key, member), (WORDS, VARIANTS), 0, 1000000)
        alleles = (uniform_pair % 1000 < rate).astype(jnp.int32) + (uniform_pair // 1000 < rate).astype(jnp.int32)
        packed = packed + alleles * 3 ** member
    packed = packed.at[0, ::7].set(728)
    return packed.astype(jnp.int32)


def set_ends(entries, own_key, least, top_value):
    index_at = [jax.random.randint(jax.random.fold_in(own_key, axis), (), 0, length) for axis, length in enumerate(entries.shape)]
    longest = entries.shape.index(max(entries.shape))
    beside = index_at[:longest] + [(index_at[longest] + 1) % entries.shape[longest]] + index_at[longest + 1:]
    return entries.at[tuple(index_at)].set(least).at[tuple(beside)].set(top_value)


def block_scale(key, shape, cuts, smallest, high):
    level, own = 1.0, jax.random.fold_in(key, 6)
    for dim, blocks in cuts:
        draws = jnp.exp(jax.random.uniform(jax.random.fold_in(own, dim), (blocks,), jnp.float32, smallest / len(cuts), high / len(cuts)))
        level = level * jnp.repeat(draws, shape[dim] // blocks).reshape([-1 if axis == dim else 1 for axis in range(len(shape))])
    return level


def centred(key, shape, spread, most, shards=(), held_as=jnp.bfloat16):
    array = jax.random.normal(key, shape, jnp.float32) * spread
    if len(shards) > 0:
        array = block_scale(key, shape, shards, -0.22, 0.18) * array
    return jnp.clip(array, min=-most, max=most).astype(held_as)


def setup_inputs(seed: int = 0) -> dict:
    key_of = jax.random.split(jax.random.key(seed), 10)
    linear_pred = centred(key_of[0], (K, PERSONS), 0.5, 3.0, ((0, 8), (1, 4)), jnp.float32)
    event_flag = set_ends((jax.random.randint(key_of[1], (PERSONS,), 0, 4) < 1).astype(jnp.int32), jax.random.fold_in(key_of[1], 1), 0, 1)
    fold_id = set_ends(jax.random.randint(key_of[2], (PERSONS,), 0, FOLDS), jax.random.fold_in(key_of[2], 1), 0, FOLDS - 1).astype(jnp.int32)
    tie_group = draw_tie_group(jax.random.fold_in(key_of[9], 71), 0)
    time_order = draw_time_order(jax.random.fold_in(key_of[9], 71), 0)
    genotypes = draw_genotypes(jax.random.fold_in(key_of[9], 71), 0)
    variant_scale = jnp.clip(jnp.exp(math.log(4.0) - 1.3862944 * jax.random.uniform(key_of[6], (VARIANTS,), jnp.float32) ** block_scale(key_of[6], (VARIANTS,), ((0, 8),), -0.2, 0.2)), 1.0, 4.0)
    penalty = jnp.clip(jnp.exp(math.log(3.0) - 2.3025851 * jax.random.uniform(key_of[7], (K,), jnp.float32) ** block_scale(key_of[7], (K,), ((0, 4),), -0.2, 0.2)), 0.3, 3.0)
    strong_set = set_ends((jax.random.randint(key_of[8], (K, VARIANTS), 0, 4) < 1).astype(jnp.int32), jax.random.fold_in(key_of[8], 1), 0, 1)
    return {"linear_pred": linear_pred, "event_flag": event_flag, "fold_id": fold_id, "tie_group": tie_group, "time_order": time_order, "genotypes": genotypes, "variant_scale": variant_scale, "penalty": penalty, "strong_set": strong_set}


def group_first(values, tie_group):
    result = values
    for offset in range(1, TIE_MAX):
        moved = jnp.pad(values, ((0, 0), (offset, 0)))[:, :-offset]
        moved_tie = jnp.pad(tie_group, (offset, 0), constant_values=-1)[:-offset]
        result = jnp.maximum(result, jnp.where((moved_tie == tie_group)[None, :], moved, jnp.zeros_like(moved)))
    return result

def group_last(values, tie_group):
    result = values
    for offset in range(1, TIE_MAX):
        moved = jnp.pad(values, ((0, 0), (0, offset)))[:, offset:]
        moved_tie = jnp.pad(tie_group, (0, offset), constant_values=-1)[offset:]
        result = jnp.maximum(result, jnp.where((moved_tie == tie_group)[None, :], moved, jnp.zeros_like(moved)))
    return result

def reference(linear_pred, event_flag, fold_id, tie_group, time_order, genotypes, variant_scale, penalty, strong_set):
    columns = jnp.arange(K, dtype=jnp.int32)
    weight = (fold_id[None, :] != (columns % FOLDS)[:, None]).astype(jnp.float32)
    events = event_flag.astype(jnp.float32)[None, :]
    risk = jnp.exp(linear_pred)
    suffix = lax.cumsum(weight * risk, axis=1, reverse=True)
    at_risk = group_first(suffix, tie_group)
    hazard = weight * events / (at_risk + 1.0 - weight)
    cumulative = group_last(jnp.cumsum(hazard, axis=1), tie_group)
    resid = (weight * (events - risk * cumulative)).astype(jnp.bfloat16)
    in_file = jnp.zeros((K, PERSONS), jnp.bfloat16).at[:, time_order].set(resid)
    words = genotypes.shape[0]
    block = math.gcd(words, 512)
    blocks = words // block
    parts = in_file.astype(jnp.float32).reshape(K, blocks, block, 6).transpose(1, 3, 0, 2)
    packed = genotypes.reshape(blocks, block, VARIANTS)

    def accumulate(total, item):
        part, words_block = item
        for member in range(6):
            dosage = (words_block // 3 ** member % 3).astype(jnp.float32)
            total = total + jnp.dot(part[member], dosage, precision=lax.Precision.HIGHEST)
        return (total, None)
    scores, _ = lax.scan(accumulate, jnp.zeros((K, VARIANTS), jnp.float32), (parts, packed))
    gradient = scores * variant_scale[None, :] / math.sqrt(PERSONS)
    violation = (1 - strong_set).astype(jnp.float32) * jnp.maximum(jnp.abs(gradient) - penalty[:, None], 0.0)
    return (gradient, violation)
```

```python
import functools
import math

import jax
import jax.numpy as jnp
from jax import lax
from jax.experimental import pallas as pl
from jax.experimental.pallas import tpu as pltpu
from jax.sharding import PartitionSpec as P

FOLDS = 8
TIE_MAX = 4
MEMBERS = 6
LANES = 128
LOW = 256
PARTS = 4
CHUNKS = 4
MESH = pl.DeviceIdType.MESH


def each(count, body):
    if count <= 8:
        for step in range(count):
            body(step)
    else:
        lax.fori_loop(0, count, lambda step, none: (body(step), none)[1], 0)


def start_all(axis, size, me, source, buffer, send, recv):
    def one(step):
        peer = lax.rem(me + step + 1, size)
        pltpu.make_async_remote_copy(
            src_ref=source(peer),
            dst_ref=buffer.at[me],
            send_sem=send.at[step],
            recv_sem=recv.at[me],
            device_id={axis: peer},
            device_id_type=MESH,
        ).start()

    each(size - 1, one)


def wait_all(axis, size, me, source, buffer, send, recv, sent):
    def one(step):
        peer = lax.rem(me + step + 1, size)
        copy = pltpu.make_async_remote_copy(
            src_ref=source(peer),
            dst_ref=buffer.at[peer],
            send_sem=send.at[step],
            recv_sem=recv.at[peer],
            device_id={axis: peer},
            device_id_type=MESH,
        )
        if sent:
            copy.wait_send()
        else:
            copy.wait_recv()

    each(size - 1, one)


def cumulate(x, reverse):
    rows, width = x.shape
    count = width // LANES
    stacked = jnp.concatenate([x[:, c * LANES : (c + 1) * LANES] for c in range(count)], axis=0)
    high = stacked.astype(jnp.bfloat16)
    rest = stacked - high.astype(jnp.float32)
    middle = rest.astype(jnp.bfloat16)
    low = (rest - middle.astype(jnp.float32)).astype(jnp.bfloat16)
    split = jnp.concatenate([high, middle, low], axis=1)
    row = lax.broadcasted_iota(jnp.int32, (3 * LANES, 2 * LANES), 0) & (LANES - 1)
    col = lax.broadcasted_iota(jnp.int32, (3 * LANES, 2 * LANES), 1)
    inside = (row >= col) if reverse else (row <= col)
    ones = jnp.where(inside | (col >= LANES), 1.0, 0.0).astype(jnp.bfloat16)
    sums = jnp.dot(split, ones, preferred_element_type=jnp.float32)
    carry = jnp.zeros((rows, LANES), jnp.float32)
    pieces = [None] * count
    for c in reversed(range(count)) if reverse else range(count):
        pieces[c] = sums[c * rows : (c + 1) * rows, :LANES] + carry
        carry = carry + sums[c * rows : (c + 1) * rows, LANES:]
    return jnp.concatenate(pieces, axis=1), carry


def over_group(values, tie, forward):
    width = values.shape[1]
    result = values
    for offset in range(1, TIE_MAX):
        by = offset if forward else width - offset
        same = pltpu.roll(tie, by, 1) == tie
        result = jnp.maximum(result, jnp.where(same, pltpu.roll(values, by, 1), 0.0))
    return result


def kernel(
    n_person,
    n_var,
    pred_ref,
    event_ref,
    fold_ref,
    tie_ref,
    order_ref,
    geno_hbm,
    scale_ref,
    penalty_ref,
    strong_ref,
    gradient_ref,
    violation_ref,
    geno,
    dosage,
    onehot,
    risk_totals,
    hazard_totals,
    outgoing,
    arrived,
    file_order,
    lhs,
    partial,
    summands,
    geno_sem,
    sems_send,
    sems_recv,
    var_send,
    var_recv,
    sum_send,
    sum_recv,
):
    f32, bf16 = jnp.float32, jnp.bfloat16
    me = lax.axis_index("person")
    here = lax.axis_index("var")
    kl, width = pred_ref.shape
    words, variants = geno.shape
    high = MEMBERS * words // LOW
    part = words // PARTS
    chunk = variants // CHUNKS
    share = gradient_ref.shape[0]

    def geno_copy(q):
        rows = pl.ds(q * part, part)
        return pltpu.make_async_copy(geno_hbm.at[rows], geno.at[rows], geno_sem.at[q])

    for q in range(PARTS):
        geno_copy(q).start()

    barrier = pltpu.get_barrier_semaphore()

    def greet(axis, size, mine):
        def one(step):
            peer = lax.rem(mine + step + 1, size)
            pl.semaphore_signal(barrier, inc=1, device_id={axis: peer}, device_id_type=MESH)

        each(size - 1, one)

    greet("person", n_person, me)
    greet("var", n_var, here)

    def decode(q):
        geno_copy(q).wait()
        piece = min(512, variants)

        def block(step, none):
            at = pl.multiple_of(q * part + step * 16, 16)
            for c in range(variants // piece):
                cols = slice(c * piece, (c + 1) * piece)
                left = geno[pl.ds(at, 16), cols].astype(f32)
                for member in range(MEMBERS):
                    if member < MEMBERS - 1:
                        above = jnp.floor(left * (1.0 / 3.0) + (1.0 / 6.0))
                        digit = left - 3.0 * above
                        left = above
                    else:
                        digit = left
                    to = pl.multiple_of(member * words + at, 16)
                    dosage[pl.ds(to, 16), cols] = digit.astype(bf16)
            return none

        lax.fori_loop(0, part // 16, block, 0)

    column = here * kl + lax.broadcasted_iota(jnp.int32, (kl, width), 0)
    weight = jnp.where(fold_ref[...] != lax.rem(column, FOLDS), 1.0, 0.0)
    events = event_ref[...].astype(f32)
    tie = jnp.broadcast_to(tie_ref[...], (kl, width))
    risk = jnp.exp(pred_ref[...])
    suffix, total = cumulate(weight * risk, True)
    risk_totals[me] = total
    pl.semaphore_wait(barrier, n_person + n_var - 2)

    def risk_source(peer):
        return risk_totals.at[me]

    def hazard_source(peer):
        return hazard_totals.at[me]

    start_all("person", n_person, me, risk_source, risk_totals, sems_send.at[0], sems_recv.at[0])

    base = over_group(suffix, tie, True) + 1.0 - weight
    numerator = weight * events
    word = jnp.floor((order_ref[...].astype(f32) + 0.5) * (1.0 / MEMBERS))
    member = order_ref[...] - MEMBERS * word.astype(jnp.int32)
    block = jnp.floor((word + 0.5) * (1.0 / words)).astype(jnp.int32)
    inner = word.astype(jnp.int32) - words * block
    upper = jnp.floor((inner.astype(f32) + 0.5) * (1.0 / LOW)).astype(jnp.int32)
    lower = inner - LOW * upper
    key = jnp.broadcast_to(block * high + member * (words // LOW) + upper, (kl, width))
    lane = lax.broadcasted_iota(jnp.int32, (LOW, LANES), 0)
    for c in range(width // LANES):
        cols = slice(c * LANES, (c + 1) * LANES)
        onehot[:, cols] = jnp.where(lane == lower[:, cols], 1.0, 0.0).astype(bf16)
    decode(0)

    wait_all("person", n_person, me, risk_source, risk_totals, sems_send.at[0], sems_recv.at[0], False)

    def carried(buffer, later):
        total = jnp.zeros((kl, LANES), f32)
        for k in range(n_person):
            at = n_person - 1 - k if later else k
            wanted = at > me if later else at < me
            total = total + jnp.where(wanted, buffer[at], 0.0)
        return jnp.concatenate([total] * (width // LANES), axis=1)

    hazard = numerator / (base + carried(risk_totals, True))
    prefix, total = cumulate(hazard, False)
    hazard_totals[me] = total
    start_all("person", n_person, me, hazard_source, hazard_totals, sems_send.at[1], sems_recv.at[1])
    last = over_group(prefix, tie, False)
    decode(1)
    wait_all("person", n_person, me, hazard_source, hazard_totals, sems_send.at[1], sems_recv.at[1], False)
    resid = weight * (events - risk * (last + carried(hazard_totals, False)))

    def for_block(to):
        first = to * high
        rows = [jnp.where(key == first + h, resid, 0.0).astype(f32) for h in range(high)]
        picked = jnp.concatenate(rows, axis=0).astype(bf16)
        return lax.dot_general(
            picked, onehot[...], (((1,), (1,)), ((), ())), preferred_element_type=f32
        ).astype(bf16)

    def out_source(peer):
        return outgoing.at[peer]

    def regroup(step):
        peer = lax.rem(me + step + 1, n_person)
        outgoing[peer] = for_block(peer)
        pltpu.make_async_remote_copy(
            src_ref=outgoing.at[peer],
            dst_ref=arrived.at[me],
            send_sem=sems_send.at[2, step],
            recv_sem=sems_recv.at[2, me],
            device_id={"person": peer},
            device_id_type=MESH,
        ).start()

    each(n_person - 1, regroup)
    arrived[me] = for_block(me)
    decode(2)
    wait_all("person", n_person, me, out_source, arrived, sems_send.at[2], sems_recv.at[2], False)
    own = arrived[0].astype(f32)
    for k in range(1, n_person):
        own = own + arrived[k].astype(f32)
    file_order[here] = own.astype(bf16)

    def file_source(peer):
        return file_order.at[here]

    start_all("var", n_var, here, file_source, file_order, var_send, var_recv)
    decode(3)
    wait_all("var", n_var, here, file_source, file_order, var_send, var_recv, False)
    gathered = [file_order[v].astype(f32) for v in range(n_var)]
    for h in range(high):
        rows = [x[h * kl : (h + 1) * kl] for x in gathered]
        lhs[:, h * LOW : (h + 1) * LOW] = jnp.concatenate(rows, axis=0).astype(bf16)

    for c in range(CHUNKS):
        def tile(step, none):
            at = pl.multiple_of(step * LOW, LOW)
            cols = pl.ds(pl.multiple_of(c * chunk + step * LOW, LOW), LOW)
            product = jnp.dot(lhs[...], dosage[:, cols], preferred_element_type=f32)
            for k in range(n_person):
                partial[c, k, :, pl.ds(at, LOW)] = product[k * share : (k + 1) * share]
            return none

        lax.fori_loop(0, chunk // LOW, tile, 0)
        summands[c, me] = partial[c, me]

        def sum_source(peer):
            return partial.at[c, peer]

        start_all("person", n_person, me, sum_source, summands.at[c], sum_send.at[c], sum_recv.at[c])

    row = lax.broadcasted_iota(jnp.int32, (share, share), 0)
    col = lax.broadcasted_iota(jnp.int32, (share, share), 1)
    penalty = jnp.sum(jnp.where(row == col, penalty_ref[...], 0.0), axis=1, keepdims=True)
    factor = 1.0 / math.sqrt(width * n_person)
    for c in range(CHUNKS):
        def sum_source(peer):
            return partial.at[c, peer]

        wait_all("person", n_person, me, sum_source, summands.at[c], sum_send.at[c], sum_recv.at[c], False)
        cols = slice(c * chunk, (c + 1) * chunk)
        mine = summands[c, 0]
        for k in range(1, n_person):
            mine = mine + summands[c, k]
        gradient = mine * (scale_ref[:, cols] * factor)
        gradient_ref[:, cols] = gradient
        violation_ref[:, cols] = (1 - strong_ref[:, cols]).astype(f32) * jnp.maximum(
            jnp.abs(gradient) - penalty, 0.0
        )

    wait_all("person", n_person, me, risk_source, risk_totals, sems_send.at[0], sems_recv.at[0], True)
    wait_all("person", n_person, me, hazard_source, hazard_totals, sems_send.at[1], sems_recv.at[1], True)
    wait_all("person", n_person, me, out_source, arrived, sems_send.at[2], sems_recv.at[2], True)
    wait_all("var", n_var, here, file_source, file_order, var_send, var_recv, True)
    for c in range(CHUNKS):
        def sum_source(peer):
            return partial.at[c, peer]

        wait_all("person", n_person, me, sum_source, summands.at[c], sum_send.at[c], sum_recv.at[c], True)


def per_device(
    n_person,
    n_var,
    linear_pred,
    event_flag,
    fold_id,
    tie_group,
    time_order,
    genotypes,
    variant_scale,
    penalty,
    strong_set,
):
    kl, width = linear_pred.shape
    words, variants = genotypes.shape
    share = strong_set.shape[0]
    columns = kl * n_var
    rows = MEMBERS * words // LOW * kl
    f32, bf16, dma = jnp.float32, jnp.bfloat16, pltpu.SemaphoreType.DMA
    vmem = pl.BlockSpec(memory_space=pltpu.VMEM)
    out = jax.ShapeDtypeStruct((share, variants), f32)
    return pl.pallas_call(
        functools.partial(kernel, n_person, n_var),
        out_shape=(out, out),
        in_specs=[vmem] * 5 + [pl.BlockSpec(memory_space=pl.ANY)] + [vmem] * 3,
        out_specs=(vmem, vmem),
        scratch_shapes=[
            pltpu.VMEM((words, variants), jnp.int32),
            pltpu.VMEM((MEMBERS * words, variants), bf16),
            pltpu.VMEM((LOW, width), bf16),
            pltpu.VMEM((n_person, kl, LANES), f32),
            pltpu.VMEM((n_person, kl, LANES), f32),
            pltpu.VMEM((n_person, rows, LOW), bf16),
            pltpu.VMEM((n_person, rows, LOW), bf16),
            pltpu.VMEM((n_var, rows, LOW), bf16),
            pltpu.VMEM((columns, MEMBERS * words), bf16),
            pltpu.VMEM((CHUNKS, n_person, share, variants // CHUNKS), f32),
            pltpu.VMEM((CHUNKS, n_person, share, variants // CHUNKS), f32),
            dma((PARTS,)),
            dma((3, n_person)),
            dma((3, n_person)),
            dma((n_var,)),
            dma((n_var,)),
            dma((CHUNKS, n_person)),
            dma((CHUNKS, n_person)),
        ],
        compiler_params=pltpu.CompilerParams(
            collective_id=0, has_side_effects=True, vmem_limit_bytes=56 * 2**20
        ),
    )(
        linear_pred,
        event_flag[None],
        fold_id[None],
        tie_group[None],
        time_order[None],
        genotypes,
        variant_scale[None],
        penalty[None],
        strong_set,
    )


def solution(mesh):
    placed = (
        P("var", "person"),
        P("person"),
        P("person"),
        P("person"),
        P("person"),
        P("person", "var"),
        P("var"),
        P("person"),
        P("person", "var"),
    )
    return jax.shard_map(
        functools.partial(per_device, mesh.shape["person"], mesh.shape["var"]),
        mesh=mesh,
        in_specs=placed,
        out_specs=(P("person", "var"), P("person", "var")),
        check_vma=False,
    )
```

```python
import functools
import math

import jax
import jax.numpy as jnp
from jax import lax
from jax.experimental import pallas as pl
from jax.experimental.pallas import tpu as pltpu
from jax.sharding import PartitionSpec as P

FOLDS = 8
TIE_MAX = 4
MEMBERS = 6
LANES = 128
LOW = 256
PARTS = 4
CHUNKS = 4
MESH = pl.DeviceIdType.MESH


def each(count, body):
    if count <= 8:
        for step in range(count):
            body(step)
    else:
        lax.fori_loop(0, count, lambda step, none: (body(step), none)[1], 0)


def start_all(axis, size, me, source, buffer, send, recv):
    def one(step):
        peer = lax.rem(me + step + 1, size)
        pltpu.make_async_remote_copy(
            src_ref=source(peer),
            dst_ref=buffer.at[me],
            send_sem=send.at[step],
            recv_sem=recv.at[me],
            device_id={axis: peer},
            device_id_type=MESH,
        ).start()

    each(size - 1, one)


def wait_all(axis, size, me, source, buffer, send, recv, sent):
    def one(step):
        peer = lax.rem(me + step + 1, size)
        copy = pltpu.make_async_remote_copy(
            src_ref=source(peer),
            dst_ref=buffer.at[peer],
            send_sem=send.at[step],
            recv_sem=recv.at[peer],
            device_id={axis: peer},
            device_id_type=MESH,
        )
        if sent:
            copy.wait_send()
        else:
            copy.wait_recv()

    each(size - 1, one)


def cumulate(x, reverse):
    rows, width = x.shape
    count = width // LANES
    stacked = jnp.concatenate([x[:, c * LANES : (c + 1) * LANES] for c in range(count)], axis=0)
    high = stacked.astype(jnp.bfloat16)
    rest = stacked - high.astype(jnp.float32)
    middle = rest.astype(jnp.bfloat16)
    low = (rest - middle.astype(jnp.float32)).astype(jnp.bfloat16)
    split = jnp.concatenate([high, middle, low], axis=1)
    row = lax.broadcasted_iota(jnp.int32, (3 * LANES, 2 * LANES), 0) & (LANES - 1)
    col = lax.broadcasted_iota(jnp.int32, (3 * LANES, 2 * LANES), 1)
    inside = (row >= col) if reverse else (row <= col)
    ones = jnp.where(inside | (col >= LANES), 1.0, 0.0).astype(jnp.bfloat16)
    sums = jnp.dot(split, ones, preferred_element_type=jnp.float32)
    carry = jnp.zeros((rows, LANES), jnp.float32)
    pieces = [None] * count
    for c in reversed(range(count)) if reverse else range(count):
        pieces[c] = sums[c * rows : (c + 1) * rows, :LANES] + carry
        carry = carry + sums[c * rows : (c + 1) * rows, LANES:]
    return jnp.concatenate(pieces, axis=1), carry


def over_group(values, tie, forward):
    width = values.shape[1]
    result = values
    for offset in range(1, TIE_MAX):
        by = offset if forward else width - offset
        same = pltpu.roll(tie, by, 1) == tie
        result = jnp.maximum(result, jnp.where(same, pltpu.roll(values, by, 1), 0.0))
    return result


def kernel(
    n_person,
    n_var,
    pred_ref,
    event_ref,
    fold_ref,
    tie_ref,
    order_ref,
    geno_hbm,
    summed_ref,
    geno,
    dosage,
    onehot,
    risk_totals,
    hazard_totals,
    outgoing,
    arrived,
    file_order,
    lhs,
    own_part,
    partial,
    summands,
    geno_sem,
    sems_send,
    sems_recv,
    var_send,
    var_recv,
    sum_send,
    sum_recv,
):
    f32, bf16 = jnp.float32, jnp.bfloat16
    me = lax.axis_index("person")
    here = lax.axis_index("var")
    kl, width = pred_ref.shape
    words, variants = geno.shape
    high = MEMBERS * words // LOW
    part = words // PARTS
    chunk = variants // CHUNKS
    share = summed_ref.shape[0]

    def geno_copy(q):
        rows = pl.ds(q * part, part)
        return pltpu.make_async_copy(geno_hbm.at[rows], geno.at[rows], geno_sem.at[q])

    for q in range(PARTS):
        geno_copy(q).start()

    barrier = pltpu.get_barrier_semaphore()

    def greet(axis, size, mine):
        def one(step):
            peer = lax.rem(mine + step + 1, size)
            pl.semaphore_signal(barrier, inc=1, device_id={axis: peer}, device_id_type=MESH)

        each(size - 1, one)

    greet("person", n_person, me)
    greet("var", n_var, here)

    def decode(q):
        geno_copy(q).wait()
        piece = min(512, variants)

        def block(step, none):
            at = pl.multiple_of(q * part + step * 16, 16)
            for c in range(variants // piece):
                cols = slice(c * piece, (c + 1) * piece)
                left = geno[pl.ds(at, 16), cols].astype(f32)
                for member in range(MEMBERS):
                    if member < MEMBERS - 1:
                        above = jnp.floor(left * (1.0 / 3.0) + (1.0 / 6.0))
                        digit = left - 3.0 * above
                        left = above
                    else:
                        digit = left
                    to = pl.multiple_of(member * words + at, 16)
                    dosage[pl.ds(to, 16), cols] = digit.astype(bf16)
            return none

        lax.fori_loop(0, part // 16, block, 0)

    column = here * kl + lax.broadcasted_iota(jnp.int32, (kl, width), 0)
    weight = jnp.where(fold_ref[...] != lax.rem(column, FOLDS), 1.0, 0.0)
    events = event_ref[...].astype(f32)
    tie = jnp.broadcast_to(tie_ref[...], (kl, width))
    risk = jnp.exp(pred_ref[...])
    suffix, total = cumulate(weight * risk, True)
    risk_totals[me] = total
    pl.semaphore_wait(barrier, n_person + n_var - 2)

    def risk_source(peer):
        return risk_totals.at[me]

    def hazard_source(peer):
        return hazard_totals.at[me]

    start_all("person", n_person, me, risk_source, risk_totals, sems_send.at[0], sems_recv.at[0])

    base = over_group(suffix, tie, True) + 1.0 - weight
    numerator = weight * events
    word = jnp.floor((order_ref[...].astype(f32) + 0.5) * (1.0 / MEMBERS))
    member = order_ref[...] - MEMBERS * word.astype(jnp.int32)
    block = jnp.floor((word + 0.5) * (1.0 / words)).astype(jnp.int32)
    inner = word.astype(jnp.int32) - words * block
    upper = jnp.floor((inner.astype(f32) + 0.5) * (1.0 / LOW)).astype(jnp.int32)
    lower = inner - LOW * upper
    key = jnp.broadcast_to(block * high + member * (words // LOW) + upper, (kl, width))
    lane = lax.broadcasted_iota(jnp.int32, (LOW, LANES), 0)
    for c in range(width // LANES):
        cols = slice(c * LANES, (c + 1) * LANES)
        onehot[:, cols] = jnp.where(lane == lower[:, cols], 1.0, 0.0).astype(bf16)
    decode(0)

    wait_all("person", n_person, me, risk_source, risk_totals, sems_send.at[0], sems_recv.at[0], False)

    def carried(buffer, later):
        total = jnp.zeros((kl, LANES), f32)
        for k in range(n_person):
            at = n_person - 1 - k if later else k
            wanted = at > me if later else at < me
            total = total + jnp.where(wanted, buffer[at], 0.0)
        return jnp.concatenate([total] * (width // LANES), axis=1)

    hazard = numerator / (base + carried(risk_totals, True))
    prefix, total = cumulate(hazard, False)
    hazard_totals[me] = total
    start_all("person", n_person, me, hazard_source, hazard_totals, sems_send.at[1], sems_recv.at[1])
    last = over_group(prefix, tie, False)
    decode(1)
    wait_all("person", n_person, me, hazard_source, hazard_totals, sems_send.at[1], sems_recv.at[1], False)
    resid = weight * (events - risk * (last + carried(hazard_totals, False)))

    def for_block(to):
        first = to * high
        rows = [jnp.where(key == first + h, resid, 0.0).astype(f32) for h in range(high)]
        picked = jnp.concatenate(rows, axis=0).astype(bf16)
        return lax.dot_general(
            picked, onehot[...], (((1,), (1,)), ((), ())), preferred_element_type=f32
        ).astype(bf16)

    def out_source(peer):
        return outgoing.at[peer]

    def regroup(step):
        peer = lax.rem(me + step + 1, n_person)
        outgoing[peer] = for_block(peer)
        pltpu.make_async_remote_copy(
            src_ref=outgoing.at[peer],
            dst_ref=arrived.at[me],
            send_sem=sems_send.at[2, step],
            recv_sem=sems_recv.at[2, me],
            device_id={"person": peer},
            device_id_type=MESH,
        ).start()

    each(n_person - 1, regroup)
    arrived[me] = for_block(me)
    decode(2)
    wait_all("person", n_person, me, out_source, arrived, sems_send.at[2], sems_recv.at[2], False)
    own = arrived[0].astype(f32)
    for k in range(1, n_person):
        own = own + arrived[k].astype(f32)
    file_order[here] = own.astype(bf16)

    def file_source(peer):
        return file_order.at[here]

    start_all("var", n_var, here, file_source, file_order, var_send, var_recv)
    decode(3)
    wait_all("var", n_var, here, file_source, file_order, var_send, var_recv, False)
    gathered = [file_order[v].astype(f32) for v in range(n_var)]
    for h in range(high):
        rows = [x[h * kl : (h + 1) * kl] for x in gathered]
        lhs[:, h * LOW : (h + 1) * LOW] = jnp.concatenate(rows, axis=0).astype(bf16)

    for c in range(CHUNKS):
        def tile(step, none):
            at = pl.multiple_of(step * LOW, LOW)
            cols = pl.ds(pl.multiple_of(c * chunk + step * LOW, LOW), LOW)
            product = jnp.dot(lhs[...], dosage[:, cols], preferred_element_type=f32)
            for k in range(n_person):
                rows = product[k * share : (k + 1) * share]
                partial[c, k, :, pl.ds(at, LOW)] = rows.astype(bf16)
                own_part[k, :, cols] = rows
            return none

        lax.fori_loop(0, chunk // LOW, tile, 0)

        def sum_source(peer):
            return partial.at[c, peer]

        start_all("person", n_person, me, sum_source, summands.at[c], sum_send.at[c], sum_recv.at[c])

    for c in range(CHUNKS):
        def sum_source(peer):
            return partial.at[c, peer]

        wait_all("person", n_person, me, sum_source, summands.at[c], sum_send.at[c], sum_recv.at[c], False)
        cols = slice(c * chunk, (c + 1) * chunk)
        mine = own_part[me, :, cols]
        for k in range(n_person):
            mine = mine + jnp.where(k == me, 0.0, summands[c, k].astype(f32))
        summed_ref[:, cols] = mine

    wait_all("person", n_person, me, risk_source, risk_totals, sems_send.at[0], sems_recv.at[0], True)
    wait_all("person", n_person, me, hazard_source, hazard_totals, sems_send.at[1], sems_recv.at[1], True)
    wait_all("person", n_person, me, out_source, arrived, sems_send.at[2], sems_recv.at[2], True)
    wait_all("var", n_var, here, file_source, file_order, var_send, var_recv, True)
    for c in range(CHUNKS):
        def sum_source(peer):
            return partial.at[c, peer]

        wait_all("person", n_person, me, sum_source, summands.at[c], sum_send.at[c], sum_recv.at[c], True)


def per_device(
    n_person,
    n_var,
    linear_pred,
    event_flag,
    fold_id,
    tie_group,
    time_order,
    genotypes,
    variant_scale,
    penalty,
    strong_set,
):
    kl, width = linear_pred.shape
    words, variants = genotypes.shape
    share = strong_set.shape[0]
    columns = kl * n_var
    rows = MEMBERS * words // LOW * kl
    f32, bf16, dma = jnp.float32, jnp.bfloat16, pltpu.SemaphoreType.DMA
    vmem = pl.BlockSpec(memory_space=pltpu.VMEM)
    summed = pl.pallas_call(
        functools.partial(kernel, n_person, n_var),
        out_shape=jax.ShapeDtypeStruct((share, variants), f32),
        in_specs=[vmem] * 5 + [pl.BlockSpec(memory_space=pl.ANY)],
        out_specs=vmem,
        scratch_shapes=[
            pltpu.VMEM((words, variants), jnp.int32),
            pltpu.VMEM((MEMBERS * words, variants), bf16),
            pltpu.VMEM((LOW, width), bf16),
            pltpu.VMEM((n_person, kl, LANES), f32),
            pltpu.VMEM((n_person, kl, LANES), f32),
            pltpu.VMEM((n_person, rows, LOW), bf16),
            pltpu.VMEM((n_person, rows, LOW), bf16),
            pltpu.VMEM((n_var, rows, LOW), bf16),
            pltpu.VMEM((columns, MEMBERS * words), bf16),
            pltpu.VMEM((n_person, share, variants), f32),
            pltpu.VMEM((CHUNKS, n_person, share, variants // CHUNKS), bf16),
            pltpu.VMEM((CHUNKS, n_person, share, variants // CHUNKS), bf16),
            dma((PARTS,)),
            dma((3, n_person)),
            dma((3, n_person)),
            dma((n_var,)),
            dma((n_var,)),
            dma((CHUNKS, n_person)),
            dma((CHUNKS, n_person)),
        ],
        compiler_params=pltpu.CompilerParams(
            collective_id=0, has_side_effects=True, vmem_limit_bytes=56 * 2**20
        ),
    )(
        linear_pred,
        event_flag[None],
        fold_id[None],
        tie_group[None],
        time_order[None],
        genotypes,
    )
    gradient = summed * (variant_scale[None, :] / math.sqrt(width * n_person))
    violation = (1 - strong_set).astype(f32) * jnp.maximum(
        jnp.abs(gradient) - penalty[:, None], 0.0
    )
    return gradient, violation


def solution(mesh):
    placed = (
        P("var", "person"),
        P("person"),
        P("person"),
        P("person"),
        P("person"),
        P("person", "var"),
        P("var"),
        P("person"),
        P("person", "var"),
    )
    return jax.shard_map(
        functools.partial(per_device, mesh.shape["person"], mesh.shape["var"]),
        mesh=mesh,
        in_specs=placed,
        out_specs=(P("person", "var"), P("person", "var")),
        check_vma=False,
    )
```

```python
import functools
import math

import jax
import jax.numpy as jnp
from jax import lax
from jax.experimental import pallas as pl
from jax.experimental.pallas import tpu as pltpu
from jax.sharding import PartitionSpec as P

FOLDS = 8
TIE_MAX = 4
MEMBERS = 6
LANES = 128
LOW = 256
PARTS = 4
CHUNKS = 4
MESH = pl.DeviceIdType.MESH


def each(count, body):
    if count <= 8:
        for step in range(count):
            body(step)
    else:
        lax.fori_loop(0, count, lambda step, none: (body(step), none)[1], 0)


def start_all(axis, size, me, source, buffer, send, recv):
    def one(step):
        peer = lax.rem(me + step + 1, size)
        pltpu.make_async_remote_copy(
            src_ref=source(peer),
            dst_ref=buffer.at[me],
            send_sem=send.at[step],
            recv_sem=recv.at[me],
            device_id={axis: peer},
            device_id_type=MESH,
        ).start()

    each(size - 1, one)


def wait_all(axis, size, me, source, buffer, send, recv, sent):
    def one(step):
        peer = lax.rem(me + step + 1, size)
        copy = pltpu.make_async_remote_copy(
            src_ref=source(peer),
            dst_ref=buffer.at[peer],
            send_sem=send.at[step],
            recv_sem=recv.at[peer],
            device_id={axis: peer},
            device_id_type=MESH,
        )
        if sent:
            copy.wait_send()
        else:
            copy.wait_recv()

    each(size - 1, one)


def cumulate(x, reverse):
    rows, width = x.shape
    count = width // LANES
    stacked = jnp.concatenate([x[:, c * LANES : (c + 1) * LANES] for c in range(count)], axis=0)
    high = stacked.astype(jnp.bfloat16)
    rest = stacked - high.astype(jnp.float32)
    middle = rest.astype(jnp.bfloat16)
    low = (rest - middle.astype(jnp.float32)).astype(jnp.bfloat16)
    split = jnp.concatenate([high, middle, low], axis=1)
    row = lax.broadcasted_iota(jnp.int32, (3 * LANES, 2 * LANES), 0) & (LANES - 1)
    col = lax.broadcasted_iota(jnp.int32, (3 * LANES, 2 * LANES), 1)
    inside = (row >= col) if reverse else (row <= col)
    ones = jnp.where(inside | (col >= LANES), 1.0, 0.0).astype(jnp.bfloat16)
    sums = jnp.dot(split, ones, preferred_element_type=jnp.float32)
    carry = jnp.zeros((rows, LANES), jnp.float32)
    pieces = [None] * count
    for c in reversed(range(count)) if reverse else range(count):
        pieces[c] = sums[c * rows : (c + 1) * rows, :LANES] + carry
        carry = carry + sums[c * rows : (c + 1) * rows, LANES:]
    return jnp.concatenate(pieces, axis=1), carry


def over_group(values, tie, forward):
    width = values.shape[1]
    result = values
    for offset in range(1, TIE_MAX):
        by = offset if forward else width - offset
        same = pltpu.roll(tie, by, 1) == tie
        result = jnp.maximum(result, jnp.where(same, pltpu.roll(values, by, 1), 0.0))
    return result


def kernel(
    n_person,
    n_var,
    pred_ref,
    event_ref,
    fold_ref,
    tie_ref,
    order_ref,
    geno_hbm,
    summed_ref,
    geno,
    dosage,
    onehot,
    risk_totals,
    hazard_totals,
    outgoing,
    arrived,
    file_order,
    lhs,
    own_part,
    partial,
    summands,
    levels,
    levels_in,
    means,
    counts,
    geno_sem,
    sems_send,
    sems_recv,
    var_send,
    var_recv,
    sum_send,
    sum_recv,
    side_send,
    side_recv,
):
    f32, bf16 = jnp.float32, jnp.bfloat16
    me = lax.axis_index("person")
    here = lax.axis_index("var")
    kl, width = pred_ref.shape
    words, variants = geno.shape
    high = MEMBERS * words // LOW
    part = words // PARTS
    chunk = variants // CHUNKS
    share = summed_ref.shape[0]

    def geno_copy(q):
        rows = pl.ds(q * part, part)
        return pltpu.make_async_copy(geno_hbm.at[rows], geno.at[rows], geno_sem.at[q])

    for q in range(PARTS):
        geno_copy(q).start()

    barrier = pltpu.get_barrier_semaphore()

    def greet(axis, size, mine):
        def one(step):
            peer = lax.rem(mine + step + 1, size)
            pl.semaphore_signal(barrier, inc=1, device_id={axis: peer}, device_id_type=MESH)

        each(size - 1, one)

    greet("person", n_person, me)
    greet("var", n_var, here)

    def decode(q):
        geno_copy(q).wait()
        piece = min(512, variants)

        def block(step, none):
            at = pl.multiple_of(q * part + step * 16, 16)
            for c in range(variants // piece):
                cols = slice(c * piece, (c + 1) * piece)
                left = geno[pl.ds(at, 16), cols].astype(f32)
                count = counts[:, cols]
                for member in range(MEMBERS):
                    if member < MEMBERS - 1:
                        above = jnp.floor(left * (1.0 / 3.0) + (1.0 / 6.0))
                        digit = left - 3.0 * above
                        left = above
                    else:
                        digit = left
                    count = count + digit
                    to = pl.multiple_of(member * words + at, 16)
                    dosage[pl.ds(to, 16), cols] = digit.astype(bf16)
                counts[:, cols] = count
            return none

        lax.fori_loop(0, part // 16, block, 0)

    column = here * kl + lax.broadcasted_iota(jnp.int32, (kl, width), 0)
    weight = jnp.where(fold_ref[...] != lax.rem(column, FOLDS), 1.0, 0.0)
    events = event_ref[...].astype(f32)
    tie = jnp.broadcast_to(tie_ref[...], (kl, width))
    risk = jnp.exp(pred_ref[...])
    suffix, total = cumulate(weight * risk, True)
    risk_totals[me] = total
    pl.semaphore_wait(barrier, n_person + n_var - 2)

    def risk_source(peer):
        return risk_totals.at[me]

    def hazard_source(peer):
        return hazard_totals.at[me]

    start_all("person", n_person, me, risk_source, risk_totals, sems_send.at[0], sems_recv.at[0])

    base = over_group(suffix, tie, True) + 1.0 - weight
    numerator = weight * events
    word = jnp.floor((order_ref[...].astype(f32) + 0.5) * (1.0 / MEMBERS))
    member = order_ref[...] - MEMBERS * word.astype(jnp.int32)
    block = jnp.floor((word + 0.5) * (1.0 / words)).astype(jnp.int32)
    inner = word.astype(jnp.int32) - words * block
    upper = jnp.floor((inner.astype(f32) + 0.5) * (1.0 / LOW)).astype(jnp.int32)
    lower = inner - LOW * upper
    key = jnp.broadcast_to(block * high + member * (words // LOW) + upper, (kl, width))
    lane = lax.broadcasted_iota(jnp.int32, (LOW, LANES), 0)
    for c in range(width // LANES):
        cols = slice(c * LANES, (c + 1) * LANES)
        onehot[:, cols] = jnp.where(lane == lower[:, cols], 1.0, 0.0).astype(bf16)
    counts[...] = jnp.zeros_like(counts)
    decode(0)

    wait_all("person", n_person, me, risk_source, risk_totals, sems_send.at[0], sems_recv.at[0], False)

    def carried(buffer, later):
        total = jnp.zeros((kl, LANES), f32)
        for k in range(n_person):
            at = n_person - 1 - k if later else k
            wanted = at > me if later else at < me
            total = total + jnp.where(wanted, buffer[at], 0.0)
        return jnp.concatenate([total] * (width // LANES), axis=1)

    hazard = numerator / (base + carried(risk_totals, True))
    prefix, total = cumulate(hazard, False)
    hazard_totals[me] = total
    start_all("person", n_person, me, hazard_source, hazard_totals, sems_send.at[1], sems_recv.at[1])
    last = over_group(prefix, tie, False)
    decode(1)
    wait_all("person", n_person, me, hazard_source, hazard_totals, sems_send.at[1], sems_recv.at[1], False)
    resid = weight * (events - risk * (last + carried(hazard_totals, False)))

    def for_block(to):
        first = to * high
        rows = [jnp.where(key == first + h, resid, 0.0).astype(f32) for h in range(high)]
        picked = jnp.concatenate(rows, axis=0).astype(bf16)
        return lax.dot_general(
            picked, onehot[...], (((1,), (1,)), ((), ())), preferred_element_type=f32
        ).astype(bf16)

    def out_source(peer):
        return outgoing.at[peer]

    def regroup(step):
        peer = lax.rem(me + step + 1, n_person)
        outgoing[peer] = for_block(peer)
        pltpu.make_async_remote_copy(
            src_ref=outgoing.at[peer],
            dst_ref=arrived.at[me],
            send_sem=sems_send.at[2, step],
            recv_sem=sems_recv.at[2, me],
            device_id={"person": peer},
            device_id_type=MESH,
        ).start()

    each(n_person - 1, regroup)
    arrived[me] = for_block(me)
    decode(2)
    wait_all("person", n_person, me, out_source, arrived, sems_send.at[2], sems_recv.at[2], False)
    own = arrived[0].astype(f32)
    for k in range(1, n_person):
        own = own + arrived[k].astype(f32)
    file_order[here] = own.astype(bf16)

    def file_source(peer):
        return file_order.at[here]

    start_all("var", n_var, here, file_source, file_order, var_send, var_recv)
    decode(3)
    means[me] = jnp.sum(counts[...], axis=0, keepdims=True) * (1.0 / (MEMBERS * words))

    def mean_source(peer):
        return means.at[me]

    start_all("person", n_person, me, mean_source, means, side_send.at[1], side_recv.at[1])
    wait_all("var", n_var, here, file_source, file_order, var_send, var_recv, False)
    gathered = [file_order[v].astype(f32) for v in range(n_var)]
    columns = n_var * kl
    level = jnp.zeros((columns, LOW), f32)
    for h in range(high):
        rows = jnp.concatenate([x[h * kl : (h + 1) * kl] for x in gathered], axis=0)
        lhs[:, h * LOW : (h + 1) * LOW] = rows.astype(bf16)
        level = level + rows
    level = jnp.sum(level, axis=1, keepdims=True)
    for k in range(n_person):
        levels[k] = jnp.broadcast_to(level[k * share : (k + 1) * share], (share, LANES))

    def level_source(peer):
        return levels.at[peer]

    start_all("person", n_person, me, level_source, levels_in, side_send.at[0], side_recv.at[0])

    for c in range(CHUNKS):
        def tile(step, none):
            at = pl.multiple_of(step * LOW, LOW)
            cols = pl.ds(pl.multiple_of(c * chunk + step * LOW, LOW), LOW)
            product = jnp.dot(lhs[...], dosage[:, cols], preferred_element_type=f32)
            mean = means[me, :, cols]
            for k in range(n_person):
                rows = product[k * share : (k + 1) * share]
                centred = rows - level[k * share : (k + 1) * share] * mean
                partial[c, k, :, pl.ds(at, LOW)] = centred.astype(bf16)
                own_part[k, :, cols] = rows
            return none

        lax.fori_loop(0, chunk // LOW, tile, 0)

        def sum_source(peer):
            return partial.at[c, peer]

        start_all("person", n_person, me, sum_source, summands.at[c], sum_send.at[c], sum_recv.at[c])

    wait_all("person", n_person, me, level_source, levels_in, side_send.at[0], side_recv.at[0], False)
    wait_all("person", n_person, me, mean_source, means, side_send.at[1], side_recv.at[1], False)
    for c in range(CHUNKS):
        def sum_source(peer):
            return partial.at[c, peer]

        wait_all("person", n_person, me, sum_source, summands.at[c], sum_send.at[c], sum_recv.at[c], False)
        cols = slice(c * chunk, (c + 1) * chunk)
        mine = own_part[me, :, cols]
        for k in range(n_person):
            other = summands[c, k].astype(f32) + levels_in[k][:, :1] * means[k, :, cols]
            mine = mine + jnp.where(k == me, 0.0, other)
        summed_ref[:, cols] = mine

    wait_all("person", n_person, me, risk_source, risk_totals, sems_send.at[0], sems_recv.at[0], True)
    wait_all("person", n_person, me, hazard_source, hazard_totals, sems_send.at[1], sems_recv.at[1], True)
    wait_all("person", n_person, me, out_source, arrived, sems_send.at[2], sems_recv.at[2], True)
    wait_all("var", n_var, here, file_source, file_order, var_send, var_recv, True)
    wait_all("person", n_person, me, level_source, levels_in, side_send.at[0], side_recv.at[0], True)
    wait_all("person", n_person, me, mean_source, means, side_send.at[1], side_recv.at[1], True)
    for c in range(CHUNKS):
        def sum_source(peer):
            return partial.at[c, peer]

        wait_all("person", n_person, me, sum_source, summands.at[c], sum_send.at[c], sum_recv.at[c], True)


def per_device(
    n_person,
    n_var,
    linear_pred,
    event_flag,
    fold_id,
    tie_group,
    time_order,
    genotypes,
    variant_scale,
    penalty,
    strong_set,
):
    kl, width = linear_pred.shape
    words, variants = genotypes.shape
    share = strong_set.shape[0]
    columns = kl * n_var
    rows = MEMBERS * words // LOW * kl
    f32, bf16, dma = jnp.float32, jnp.bfloat16, pltpu.SemaphoreType.DMA
    vmem = pl.BlockSpec(memory_space=pltpu.VMEM)
    summed = pl.pallas_call(
        functools.partial(kernel, n_person, n_var),
        out_shape=jax.ShapeDtypeStruct((share, variants), f32),
        in_specs=[vmem] * 5 + [pl.BlockSpec(memory_space=pl.ANY)],
        out_specs=vmem,
        scratch_shapes=[
            pltpu.VMEM((words, variants), jnp.int32),
            pltpu.VMEM((MEMBERS * words, variants), bf16),
            pltpu.VMEM((LOW, width), bf16),
            pltpu.VMEM((n_person, kl, LANES), f32),
            pltpu.VMEM((n_person, kl, LANES), f32),
            pltpu.VMEM((n_person, rows, LOW), bf16),
            pltpu.VMEM((n_person, rows, LOW), bf16),
            pltpu.VMEM((n_var, rows, LOW), bf16),
            pltpu.VMEM((columns, MEMBERS * words), bf16),
            pltpu.VMEM((n_person, share, variants), f32),
            pltpu.VMEM((CHUNKS, n_person, share, variants // CHUNKS), bf16),
            pltpu.VMEM((CHUNKS, n_person, share, variants // CHUNKS), bf16),
            pltpu.VMEM((n_person, share, LANES), f32),
            pltpu.VMEM((n_person, share, LANES), f32),
            pltpu.VMEM((n_person, 1, variants), f32),
            pltpu.VMEM((16, variants), f32),
            dma((PARTS,)),
            dma((3, n_person)),
            dma((3, n_person)),
            dma((n_var,)),
            dma((n_var,)),
            dma((CHUNKS, n_person)),
            dma((CHUNKS, n_person)),
            dma((2, n_person)),
            dma((2, n_person)),
        ],
        compiler_params=pltpu.CompilerParams(
            collective_id=0, has_side_effects=True, vmem_limit_bytes=56 * 2**20
        ),
    )(
        linear_pred,
        event_flag[None],
        fold_id[None],
        tie_group[None],
        time_order[None],
        genotypes,
    )
    gradient = summed * variant_scale[None, :] * (1.0 / math.sqrt(width * n_person))
    violation = (1 - strong_set).astype(f32) * jnp.maximum(
        jnp.abs(gradient) - penalty[:, None], 0.0
    )
    return gradient, violation


def solution(mesh):
    placed = (
        P("var", "person"),
        P("person"),
        P("person"),
        P("person"),
        P("person"),
        P("person", "var"),
        P("var"),
        P("person"),
        P("person", "var"),
    )
    return jax.shard_map(
        functools.partial(per_device, mesh.shape["person"], mesh.shape["var"]),
        mesh=mesh,
        in_specs=placed,
        out_specs=(P("person", "var"), P("person", "var")),
        check_vma=False,
    )
```

```python
import functools
import math

import jax
import jax.numpy as jnp
from jax import lax
from jax.experimental import pallas as pl
from jax.experimental.pallas import tpu as pltpu
from jax.sharding import PartitionSpec as P

FOLDS = 8
TIE_MAX = 4
MEMBERS = 6
LANES = 128
LOW = 256
TILE = 512
PARTS = 4
CHUNKS = 4
MESH = pl.DeviceIdType.MESH


def each(count, body):
    if count <= 8:
        for step in range(count):
            body(step)
    else:
        lax.fori_loop(0, count, lambda step, none: (body(step), none)[1], 0)


def start_all(axis, size, me, source, buffer, send, recv):
    def one(step):
        peer = lax.rem(me + step + 1, size)
        pltpu.make_async_remote_copy(
            src_ref=source(peer),
            dst_ref=buffer.at[me],
            send_sem=send.at[step],
            recv_sem=recv.at[me],
            device_id={axis: peer},
            device_id_type=MESH,
        ).start()

    each(size - 1, one)


def wait_all(axis, size, me, source, buffer, send, recv, sent):
    def one(step):
        peer = lax.rem(me + step + 1, size)
        copy = pltpu.make_async_remote_copy(
            src_ref=source(peer),
            dst_ref=buffer.at[peer],
            send_sem=send.at[step],
            recv_sem=recv.at[peer],
            device_id={axis: peer},
            device_id_type=MESH,
        )
        if sent:
            copy.wait_send()
        else:
            copy.wait_recv()

    each(size - 1, one)


def cumulate(x, reverse):
    rows, width = x.shape
    count = width // LANES
    stacked = jnp.concatenate([x[:, c * LANES : (c + 1) * LANES] for c in range(count)], axis=0)
    high = stacked.astype(jnp.bfloat16)
    rest = stacked - high.astype(jnp.float32)
    middle = rest.astype(jnp.bfloat16)
    low = (rest - middle.astype(jnp.float32)).astype(jnp.bfloat16)
    split = jnp.concatenate([high, middle, low], axis=1)
    row = lax.broadcasted_iota(jnp.int32, (3 * LANES, 2 * LANES), 0) & (LANES - 1)
    col = lax.broadcasted_iota(jnp.int32, (3 * LANES, 2 * LANES), 1)
    inside = (row >= col) if reverse else (row <= col)
    ones = jnp.where(inside | (col >= LANES), 1.0, 0.0).astype(jnp.bfloat16)
    sums = jnp.dot(split, ones, preferred_element_type=jnp.float32)
    carry = jnp.zeros((rows, LANES), jnp.float32)
    pieces = [None] * count
    for c in reversed(range(count)) if reverse else range(count):
        pieces[c] = sums[c * rows : (c + 1) * rows, :LANES] + carry
        carry = carry + sums[c * rows : (c + 1) * rows, LANES:]
    return jnp.concatenate(pieces, axis=1), carry


def over_group(values, tie, forward):
    width = values.shape[1]
    result = values
    for offset in range(1, TIE_MAX):
        by = offset if forward else width - offset
        same = pltpu.roll(tie, by, 1) == tie
        result = jnp.maximum(result, jnp.where(same, pltpu.roll(values, by, 1), 0.0))
    return result


def kernel(
    n_person,
    n_var,
    pred_ref,
    event_ref,
    fold_ref,
    tie_ref,
    order_ref,
    geno_hbm,
    summed_ref,
    geno,
    dosage,
    onehot,
    risk_totals,
    hazard_totals,
    outgoing,
    arrived,
    file_order,
    lhs,
    own_part,
    partial,
    summands,
    levels,
    levels_in,
    means,
    counts,
    geno_sem,
    sems_send,
    sems_recv,
    var_send,
    var_recv,
    sum_send,
    sum_recv,
    side_send,
    side_recv,
):
    f32, bf16 = jnp.float32, jnp.bfloat16
    me = lax.axis_index("person")
    here = lax.axis_index("var")
    kl, width = pred_ref.shape
    words, variants = geno.shape
    high = MEMBERS * words // LOW
    part = words // PARTS
    chunk = variants // CHUNKS
    share = summed_ref.shape[0]

    def geno_copy(q):
        rows = pl.ds(q * part, part)
        return pltpu.make_async_copy(geno_hbm.at[rows], geno.at[rows], geno_sem.at[q])

    for q in range(PARTS):
        geno_copy(q).start()

    barrier = pltpu.get_barrier_semaphore()

    def greet(axis, size, mine):
        def one(step):
            peer = lax.rem(mine + step + 1, size)
            pl.semaphore_signal(barrier, inc=1, device_id={axis: peer}, device_id_type=MESH)

        each(size - 1, one)

    greet("person", n_person, me)
    greet("var", n_var, here)

    def decode(q):
        geno_copy(q).wait()
        piece = min(512, variants)

        def block(step, none):
            at = pl.multiple_of(q * part + step * 16, 16)
            for c in range(variants // piece):
                cols = slice(c * piece, (c + 1) * piece)
                left = geno[pl.ds(at, 16), cols].astype(f32)
                count = counts[:, cols]
                for member in range(MEMBERS):
                    if member < MEMBERS - 1:
                        above = jnp.floor(left * (1.0 / 3.0) + (1.0 / 6.0))
                        digit = left - 3.0 * above
                        left = above
                    else:
                        digit = left
                    count = count + digit
                    to = pl.multiple_of(member * words + at, 16)
                    dosage[pl.ds(to, 16), cols] = digit.astype(bf16)
                counts[:, cols] = count
            return none

        lax.fori_loop(0, part // 16, block, 0)

    column = here * kl + lax.broadcasted_iota(jnp.int32, (kl, width), 0)
    weight = jnp.where(fold_ref[...] != lax.rem(column, FOLDS), 1.0, 0.0)
    events = event_ref[...].astype(f32)
    tie = jnp.broadcast_to(tie_ref[...], (kl, width))
    risk = jnp.exp(pred_ref[...])
    suffix, total = cumulate(weight * risk, True)
    risk_totals[me] = total
    pl.semaphore_wait(barrier, n_person + n_var - 2)

    def risk_source(peer):
        return risk_totals.at[me]

    def hazard_source(peer):
        return hazard_totals.at[me]

    start_all("person", n_person, me, risk_source, risk_totals, sems_send.at[0], sems_recv.at[0])

    base = over_group(suffix, tie, True) + 1.0 - weight
    numerator = weight * events
    word = jnp.floor((order_ref[...].astype(f32) + 0.5) * (1.0 / MEMBERS))
    member = order_ref[...] - MEMBERS * word.astype(jnp.int32)
    block = jnp.floor((word + 0.5) * (1.0 / words)).astype(jnp.int32)
    inner = word.astype(jnp.int32) - words * block
    upper = jnp.floor((inner.astype(f32) + 0.5) * (1.0 / LOW)).astype(jnp.int32)
    lower = inner - LOW * upper
    key = jnp.broadcast_to(block * high + member * (words // LOW) + upper, (kl, width))
    lane = lax.broadcasted_iota(jnp.int32, (LOW, LANES), 0)
    for c in range(width // LANES):
        cols = slice(c * LANES, (c + 1) * LANES)
        onehot[:, cols] = jnp.where(lane == lower[:, cols], 1.0, 0.0).astype(bf16)
    counts[...] = jnp.zeros_like(counts)
    decode(0)

    wait_all("person", n_person, me, risk_source, risk_totals, sems_send.at[0], sems_recv.at[0], False)

    def carried(buffer, later):
        total = jnp.zeros((kl, LANES), f32)
        for k in range(n_person):
            at = n_person - 1 - k if later else k
            wanted = at > me if later else at < me
            total = total + jnp.where(wanted, buffer[at], 0.0)
        return jnp.concatenate([total] * (width // LANES), axis=1)

    hazard = numerator / (base + carried(risk_totals, True))
    prefix, total = cumulate(hazard, False)
    hazard_totals[me] = total
    start_all("person", n_person, me, hazard_source, hazard_totals, sems_send.at[1], sems_recv.at[1])
    last = over_group(prefix, tie, False)
    decode(1)
    wait_all("person", n_person, me, hazard_source, hazard_totals, sems_send.at[1], sems_recv.at[1], False)
    resid = weight * (events - risk * (last + carried(hazard_totals, False)))

    def for_block(to):
        first = to * high
        rows = [jnp.where(key == first + h, resid, 0.0).astype(f32) for h in range(high)]
        picked = jnp.concatenate(rows, axis=0).astype(bf16)
        return lax.dot_general(
            picked, onehot[...], (((1,), (1,)), ((), ())), preferred_element_type=f32
        ).astype(bf16)

    def out_source(peer):
        return outgoing.at[peer]

    def regroup(step):
        peer = lax.rem(me + step + 1, n_person)
        outgoing[peer] = for_block(peer)
        pltpu.make_async_remote_copy(
            src_ref=outgoing.at[peer],
            dst_ref=arrived.at[me],
            send_sem=sems_send.at[2, step],
            recv_sem=sems_recv.at[2, me],
            device_id={"person": peer},
            device_id_type=MESH,
        ).start()

    each(n_person - 1, regroup)
    arrived[me] = for_block(me)
    decode(2)
    wait_all("person", n_person, me, out_source, arrived, sems_send.at[2], sems_recv.at[2], False)
    own = arrived[0].astype(f32)
    for k in range(1, n_person):
        own = own + arrived[k].astype(f32)
    file_order[here] = own.astype(bf16)

    def file_source(peer):
        return file_order.at[here]

    start_all("var", n_var, here, file_source, file_order, var_send, var_recv)
    decode(3)
    means[me] = jnp.sum(counts[...], axis=0, keepdims=True) * (1.0 / (MEMBERS * words))

    def mean_source(peer):
        return means.at[me]

    start_all("person", n_person, me, mean_source, means, side_send.at[1], side_recv.at[1])
    wait_all("var", n_var, here, file_source, file_order, var_send, var_recv, False)
    gathered = [file_order[v].astype(f32) for v in range(n_var)]
    columns = n_var * kl
    level = jnp.zeros((columns, LOW), f32)
    for h in range(high):
        rows = jnp.concatenate([x[h * kl : (h + 1) * kl] for x in gathered], axis=0)
        lhs[:, h * LOW : (h + 1) * LOW] = rows.astype(bf16)
        level = level + rows
    level = jnp.sum(level, axis=1, keepdims=True)
    for k in range(n_person):
        levels[k] = jnp.broadcast_to(level[k * share : (k + 1) * share], (share, LANES))

    def level_source(peer):
        return levels.at[peer]

    start_all("person", n_person, me, level_source, levels_in, side_send.at[0], side_recv.at[0])

    for c in range(CHUNKS):
        def tile(step, none):
            at = pl.multiple_of(step * TILE, TILE)
            cols = pl.ds(pl.multiple_of(c * chunk + step * TILE, TILE), TILE)
            product = jnp.dot(lhs[...], dosage[:, cols], preferred_element_type=f32)
            mean = means[me, :, cols]
            for k in range(n_person):
                rows = product[k * share : (k + 1) * share]
                centred = rows - level[k * share : (k + 1) * share] * mean
                partial[c, k, :, pl.ds(at, TILE)] = centred.astype(bf16)
                own_part[k, :, cols] = rows
            return none

        lax.fori_loop(0, chunk // TILE, tile, 0)

        def sum_source(peer):
            return partial.at[c, peer]

        start_all("person", n_person, me, sum_source, summands.at[c], sum_send.at[c], sum_recv.at[c])

    wait_all("person", n_person, me, level_source, levels_in, side_send.at[0], side_recv.at[0], False)
    wait_all("person", n_person, me, mean_source, means, side_send.at[1], side_recv.at[1], False)
    for c in range(CHUNKS):
        def sum_source(peer):
            return partial.at[c, peer]

        wait_all("person", n_person, me, sum_source, summands.at[c], sum_send.at[c], sum_recv.at[c], False)
        cols = slice(c * chunk, (c + 1) * chunk)
        mine = own_part[me, :, cols]
        for k in range(n_person):
            other = summands[c, k].astype(f32) + levels_in[k][:, :1] * means[k, :, cols]
            mine = mine + jnp.where(k == me, 0.0, other)
        summed_ref[:, cols] = mine

    wait_all("person", n_person, me, risk_source, risk_totals, sems_send.at[0], sems_recv.at[0], True)
    wait_all("person", n_person, me, hazard_source, hazard_totals, sems_send.at[1], sems_recv.at[1], True)
    wait_all("person", n_person, me, out_source, arrived, sems_send.at[2], sems_recv.at[2], True)
    wait_all("var", n_var, here, file_source, file_order, var_send, var_recv, True)
    wait_all("person", n_person, me, level_source, levels_in, side_send.at[0], side_recv.at[0], True)
    wait_all("person", n_person, me, mean_source, means, side_send.at[1], side_recv.at[1], True)
    for c in range(CHUNKS):
        def sum_source(peer):
            return partial.at[c, peer]

        wait_all("person", n_person, me, sum_source, summands.at[c], sum_send.at[c], sum_recv.at[c], True)


def per_device(
    n_person,
    n_var,
    linear_pred,
    event_flag,
    fold_id,
    tie_group,
    time_order,
    genotypes,
    variant_scale,
    penalty,
    strong_set,
):
    kl, width = linear_pred.shape
    words, variants = genotypes.shape
    share = strong_set.shape[0]
    columns = kl * n_var
    rows = MEMBERS * words // LOW * kl
    f32, bf16, dma = jnp.float32, jnp.bfloat16, pltpu.SemaphoreType.DMA
    vmem = pl.BlockSpec(memory_space=pltpu.VMEM)
    summed = pl.pallas_call(
        functools.partial(kernel, n_person, n_var),
        out_shape=jax.ShapeDtypeStruct((share, variants), f32),
        in_specs=[vmem] * 5 + [pl.BlockSpec(memory_space=pl.ANY)],
        out_specs=vmem,
        scratch_shapes=[
            pltpu.VMEM((words, variants), jnp.int32),
            pltpu.VMEM((MEMBERS * words, variants), bf16),
            pltpu.VMEM((LOW, width), bf16),
            pltpu.VMEM((n_person, kl, LANES), f32),
            pltpu.VMEM((n_person, kl, LANES), f32),
            pltpu.VMEM((n_person, rows, LOW), bf16),
            pltpu.VMEM((n_person, rows, LOW), bf16),
            pltpu.VMEM((n_var, rows, LOW), bf16),
            pltpu.VMEM((columns, MEMBERS * words), bf16),
            pltpu.VMEM((n_person, share, variants), f32),
            pltpu.VMEM((CHUNKS, n_person, share, variants // CHUNKS), bf16),
            pltpu.VMEM((CHUNKS, n_person, share, variants // CHUNKS), bf16),
            pltpu.VMEM((n_person, share, LANES), f32),
            pltpu.VMEM((n_person, share, LANES), f32),
            pltpu.VMEM((n_person, 1, variants), f32),
            pltpu.VMEM((16, variants), f32),
            dma((PARTS,)),
            dma((3, n_person)),
            dma((3, n_person)),
            dma((n_var,)),
            dma((n_var,)),
            dma((CHUNKS, n_person)),
            dma((CHUNKS, n_person)),
            dma((2, n_person)),
            dma((2, n_person)),
        ],
        compiler_params=pltpu.CompilerParams(
            collective_id=0, has_side_effects=True, vmem_limit_bytes=56 * 2**20
        ),
    )(
        linear_pred,
        event_flag[None],
        fold_id[None],
        tie_group[None],
        time_order[None],
        genotypes,
    )
    gradient = summed * variant_scale[None, :] * (1.0 / math.sqrt(width * n_person))
    violation = (1 - strong_set).astype(f32) * jnp.maximum(
        jnp.abs(gradient) - penalty[:, None], 0.0
    )
    return gradient, violation


def solution(mesh):
    placed = (
        P("var", "person"),
        P("person"),
        P("person"),
        P("person"),
        P("person"),
        P("person", "var"),
        P("var"),
        P("person"),
        P("person", "var"),
    )
    return jax.shard_map(
        functools.partial(per_device, mesh.shape["person"], mesh.shape["var"]),
        mesh=mesh,
        in_specs=placed,
        out_specs=(P("person", "var"), P("person", "var")),
        check_vma=False,
    )
```
